32 devices in a mesh: ctx: 4 (over y, core), exp: 8 (over z, x).
Axes of the slice: x: 2, y: 2, z: 4, core: 2. Of those that a mesh axis runs over, the one named last changes fastest.
Arguments:
- residual: bfloat16 [8, 512, 7168], P('exp', 'ctx'), may hold values from -6 to 6
- queries: bfloat16 [8, 512, 1024], P('exp', 'ctx'), may hold values from -64 to 64
- latent: bfloat16 [8, 512, 512], P('exp', 'ctx'), may hold values from -6 to 6
- out_proj: bfloat16 [1024, 7168], P('ctx'), may hold values from -0.5 to 0.5
- up_weight: bfloat16 [8, 7168, 1024], P('exp', 'ctx'), may hold values from -0.0625 to 0.0625
- down_weight: bfloat16 [8, 1024, 7168], P('exp', None, 'ctx'), may hold values from -0.1875 to 0.1875
- cotangent: bfloat16 [8, 512, 7168], P('exp', 'ctx'), may hold values from -6 to 6
- routes: int32 [8, 512, 8], P('exp', 'ctx'), may hold values from 0 to 255, as said below
- gate_values: float32 [8, 512, 8], P('exp', 'ctx'), may hold values from 0.2 to 1
- documents: int32 [8, 4], P('exp'), may hold values from 0 to 2, never falling along the last dimension, each value on 1 to 2 neighbouring positions
Outputs:
- layer_out: bfloat16 [8, 512, 7168], P('exp', 'ctx')
- input_grad: bfloat16 [8, 512, 7168], P('exp', 'ctx')
- up_grad: bfloat16 [8, 7168, 1024], P('exp', 'ctx')
- down_grad: bfloat16 [8, 1024, 7168], P('exp', None, 'ctx')
The draws below stay inside these ranges and needn't reach their ends.
Inputs may be any that keep to these rules, and one draw needn't show every extreme that they name: Each token's 8 experts differ. Within one block of 128 consecutive tokens of a sequence at most 4 routes name one expert below 8, and in every draw some expert below 8 is named by exactly 4 routes of every such block. `documents`: document numbers never fall along a sequence; a document covers 1 to 2 consecutive blocks, and one covers exactly 2.
All inputs are finite; a program needn't handle non-finite values.
Results may differ from the reference program's by a relative error of at most 0.025.
Values may be sent and summed in bfloat16 or wider, within the bound.
A program may use at most 128 MiB of HBM per device.

```python
import math
import jax
import jax.numpy as jnp
import numpy as np
from jax import lax

D = 7168
FF = 1024
ALL_EXPERTS = 256
TOP = 8
LAT = 512
HEADS = 2
CAP = 4
BLOCK = 128
DOCS = 3
TOK_DEV = 128
LEN = 512
SEQS = 8
EXPERTS = 8
NBLK = 4
DOC_MAX = 2


def latent_pair(key):
    folded = jax.random.fold_in(key, 7)
    key_lat, key_query = jax.random.split(folded, 2)
    latent_draw = jax.random.normal(key_lat, (SEQS, LEN, LAT), jnp.float32)
    query_draw = jax.random.normal(key_query, (SEQS, LEN, HEADS, LAT), jnp.float32)
    latent_draw = jnp.clip(latent_draw, -6.0, 6.0)
    query_draw = jnp.clip(query_draw, -64.0, 64.0)
    return (query_draw.reshape(SEQS, LEN, HEADS * LAT), latent_draw)


def draw_queries(key, part):
    return latent_pair(key)[0].astype(jnp.bfloat16)


def draw_latent(key, part):
    return latent_pair(key)[1].astype(jnp.bfloat16)


def draw_routes(key, part):
    folded = jax.random.fold_in(key, 3)
    key_count, key_hot, key_perm, key_fill, key_roll = jax.random.split(folded, 5)
    blocks = SEQS * LEN // TOK_DEV
    counts = jax.random.randint(key_count, (blocks, EXPERTS), 0, CAP + 1)
    hottest = jax.random.randint(key_hot, (), 0, EXPERTS)
    experts_iota = jnp.arange(EXPERTS)
    counts = jnp.where(experts_iota[None, :] == hottest, CAP, counts)

    def shuffle_one(subkey):
        return jax.random.permutation(subkey, TOK_DEV)
    orders = jax.vmap(shuffle_one)(jax.random.split(key_perm, blocks))
    places = jnp.argsort(orders, axis=-1, stable=True)
    offset = (places[:, :, None] - experts_iota[None, None, :] * CAP) % TOK_DEV
    member = offset < counts[:, None, :]
    ranked = jnp.argsort(jnp.where(member, experts_iota, EXPERTS + experts_iota), axis=-1, stable=True)[:, :, :TOP]
    member_count = jnp.sum(member.astype(jnp.int32), axis=-1)
    spare = ALL_EXPERTS - EXPERTS
    start_at = jax.random.randint(key_fill, (blocks, TOK_DEV, 1), 0, spare)
    slots_iota = jnp.arange(TOP)
    filler = EXPERTS + (start_at + slots_iota * (spare // TOP)) % spare
    chosen = jnp.where(slots_iota[None, None, :] < member_count[:, :, None], ranked, filler)
    rotation = jax.random.randint(key_roll, (blocks, TOK_DEV, 1), 0, TOP)
    chosen = jnp.take_along_axis(chosen, (slots_iota[None, None, :] + rotation) % TOP, axis=-1)
    return chosen.reshape(SEQS, LEN, TOP).astype(jnp.int32)


def levels(key, shape, cuts, smallest, high):
    def one(axis_at, parts):
        draws = jax.random.uniform(jax.random.fold_in(jax.random.fold_in(key, 6), axis_at), (parts,), jnp.float32, smallest / len(cuts), high / len(cuts))
        return jnp.repeat(jnp.exp(draws), shape[axis_at] // parts).reshape((-1,) + (1,) * (len(shape) - axis_at - 1))

    gain = one(*cuts[0])
    for cut in cuts[1:]:
        gain = gain * one(*cut)
    return gain


def profile(amount, total, most, lean):
    portions = [(1 << 20) // math.isqrt(standing ** lean) + 1 for standing in range(2, amount + 1)]
    spare, given = total - most - (amount - 1), [1] * (amount - 1)
    while spare > 0:
        candidates = [i for i in range(amount - 1) if given[i] < most]
        mass, budget = sum([portions[i] for i in candidates]), spare
        for i in candidates:
            more = min(most - given[i], max(1, budget * portions[i] // mass), spare)
            given[i] = given[i] + more
            spare = spare - more
    return np.array([most] + given)


def uneven_parts(key, amount, total, bound, skew):
    if amount == 2:
        one = jax.random.randint(key, (), max(1, total - bound), min(bound, total - 1) + 1)
        return jnp.stack([one, total - one])
    tallies = jnp.asarray(profile(amount, total, bound, skew), jnp.int32)
    twos = (amount - 1) // 2
    giver, receiver = tallies[1:1 + 2 * twos:2], tallies[2:2 + 2 * twos:2]
    slack = jnp.minimum(giver - 1, bound - receiver)
    moved = jax.random.randint(jax.random.fold_in(key, 1), (twos,), 0, 1 << 20) % (slack + 1)
    tallies = tallies.at[1:1 + 2 * twos:2].set(giver - moved).at[2:2 + 2 * twos:2].set(receiver + moved)
    return tallies[jax.random.permutation(jax.random.fold_in(key, 2), amount)]


def bell_draw(key, dims, scale, most, shards=(), kind=jnp.bfloat16):
    entries = scale * jax.random.normal(key, dims, jnp.float32)
    if shards:
        entries = entries * levels(key, dims, shards, -0.22, 0.18)
    return jnp.clip(entries, -most, most).astype(kind)


def setup_inputs(seed: int = 0) -> dict:
    arg_keys = jax.random.split(jax.random.key(seed), 11)
    return {
        "residual": bell_draw(arg_keys[0], (SEQS, LEN, D), 1.0, 6.0, ((0, 8), (1, 4))),
        "queries": draw_queries(jax.random.fold_in(arg_keys[10], 71), 0),
        "latent": draw_latent(jax.random.fold_in(arg_keys[10], 71), 0),
        "out_proj": bell_draw(arg_keys[3], (HEADS * LAT, D), (HEADS * LAT // 8) ** -0.5, 0.5, ((0, 4),)),
        "up_weight": bell_draw(arg_keys[4], (EXPERTS, D, FF), D ** -0.5, 0.0625, ((0, 8), (1, 4))),
        "down_weight": bell_draw(arg_keys[5], (EXPERTS, FF, D), FF ** -0.5, 0.1875, ((0, 8), (2, 4))),
        "cotangent": bell_draw(arg_keys[6], (SEQS, LEN, D), 1.0, 6.0, ((0, 8), (1, 4))),
        "routes": draw_routes(jax.random.fold_in(arg_keys[10], 71), 0),
        "gate_values": jnp.clip(0.2 + 0.8 * jax.random.uniform(arg_keys[8], (SEQS, LEN, TOP), jnp.float32) ** levels(arg_keys[8], (SEQS, LEN, TOP), ((0, 8), (1, 4)), -0.2, 0.2), 0.2, 1.0),
        "documents": jax.vmap(lambda own: jnp.searchsorted(jnp.cumsum(uneven_parts(own, DOCS, NBLK, DOC_MAX, 2)), jnp.arange(NBLK), side="right"))(jax.random.split(arg_keys[9], SEQS)).reshape((SEQS, NBLK)).astype(jnp.int32),
    }


def silu_grad(values_in):
    sigmoid_of = jax.nn.sigmoid(values_in)
    return sigmoid_of * (1.0 + values_in * (1.0 - sigmoid_of))

def slot_tables(route_rows, gate_rows):
    experts = jnp.arange(EXPERTS, dtype=jnp.int32)
    onehot = (route_rows[:, :, None] == experts[None, None, :]).astype(jnp.int32)
    flat_hits = onehot.reshape(-1, EXPERTS)
    before = jnp.cumsum(flat_hits, axis=0) - flat_hits
    rank_in = lax.optimization_barrier(jnp.sum(before * flat_hits, axis=1)).reshape(route_rows.shape)
    valid = route_rows < EXPERTS
    slot_index = jnp.where(valid, route_rows * CAP + rank_in, -1)
    slots_all = jnp.arange(EXPERTS * CAP, dtype=jnp.int32)
    slot_hits = slot_index[None, :, :] == slots_all[:, None, None]
    picker = lax.optimization_barrier(jnp.sum(slot_hits.astype(jnp.float32), axis=2))
    weigher = lax.optimization_barrier(jnp.sum(jnp.where(slot_hits, gate_rows[None, :, :], 0.0), axis=2))
    return (picker, weigher)

def reference(residual, queries, latent, out_proj, up_weight, down_weight, cotangent, routes, gate_values, documents):
    inv_root = 1.0 / math.sqrt(LAT)

    def attend(inputs):
        query_seq, latent_seq, doc_seq = inputs
        query_f = query_seq.astype(jnp.float32).reshape(LEN, HEADS, LAT)
        latent_f = latent_seq.astype(jnp.float32)
        scores = jnp.einsum('ihk,jk->hij', query_f, latent_f) * inv_root
        positions = jnp.arange(LEN, dtype=jnp.int32)
        owner_doc = doc_seq[positions // BLOCK]
        allowed = (owner_doc[None, :] == owner_doc[:, None]) & (positions[None, :] <= positions[:, None])
        scores = jnp.where(allowed[None, :, :], scores, -jnp.inf)
        largest = lax.optimization_barrier(jnp.max(scores, axis=2, keepdims=True))
        exponent = jnp.where(allowed[None, :, :], jnp.exp(scores - largest), 0.0)
        total_sum = lax.optimization_barrier(jnp.sum(exponent, axis=2))
        rounded = lax.optimization_barrier(exponent.astype(jnp.bfloat16)).astype(jnp.float32)
        mixed_rows = jnp.einsum('hij,jk->ihk', rounded, latent_f) / jnp.transpose(total_sum)[:, :, None]
        return mixed_rows.astype(jnp.bfloat16).reshape(LEN, HEADS * LAT)
    heads_out = lax.map(attend, (queries, latent, documents))
    projected = jnp.dot(heads_out.reshape(SEQS * LEN, HEADS * LAT), out_proj, preferred_element_type=jnp.float32)
    hidden_in = (residual.reshape(SEQS * LEN, D).astype(jnp.float32) + projected).astype(jnp.bfloat16)
    blocks = SEQS * LEN // TOK_DEV
    hidden_blocks = hidden_in.reshape(blocks, TOK_DEV, D)
    cot_blocks = cotangent.reshape(blocks, TOK_DEV, D)
    route_blocks = routes.reshape(blocks, TOK_DEV, TOP)
    gate_blocks = gate_values.reshape(blocks, TOK_DEV, TOP)

    def dispatch_block(inputs):
        hidden_rows, cot_rows, route_rows, gate_rows = inputs
        picker, weigher = slot_tables(route_rows, gate_rows)
        picker_half = picker.astype(jnp.bfloat16)
        slot_gate = lax.optimization_barrier(jnp.sum(weigher, axis=1))
        slot_in = jnp.dot(picker_half, hidden_rows, preferred_element_type=jnp.float32).astype(jnp.bfloat16)
        slot_cot = (jnp.dot(picker_half, cot_rows, preferred_element_type=jnp.float32) * slot_gate[:, None]).astype(jnp.bfloat16)
        return (slot_in, slot_cot, picker, weigher)
    slot_in, slot_cot, pickers, weighers = lax.map(dispatch_block, (hidden_blocks, cot_blocks, route_blocks, gate_blocks))
    in_by_expert = slot_in.reshape(blocks, EXPERTS, CAP, D).transpose(1, 0, 2, 3).reshape(EXPERTS, blocks * CAP, D)
    cot_by_expert = slot_cot.reshape(blocks, EXPERTS, CAP, D).transpose(1, 0, 2, 3).reshape(EXPERTS, blocks * CAP, D)

    def expert(inputs):
        in_rows, cot_rows, up_part, down_part = inputs
        pre = jnp.dot(in_rows, up_part, preferred_element_type=jnp.float32)
        activated = jax.nn.silu(pre).astype(jnp.bfloat16)
        slot_out = jnp.dot(activated, down_part, preferred_element_type=jnp.float32).astype(jnp.bfloat16)
        down_grad = jnp.dot(activated.T, cot_rows, preferred_element_type=jnp.float32).astype(jnp.bfloat16)
        act_grad = jnp.dot(cot_rows, down_part.T, preferred_element_type=jnp.float32)
        pre_grad = (act_grad * silu_grad(pre)).astype(jnp.bfloat16)
        up_grad = jnp.dot(in_rows.T, pre_grad, preferred_element_type=jnp.float32).astype(jnp.bfloat16)
        slot_in_grad = jnp.dot(pre_grad, up_part.T, preferred_element_type=jnp.float32).astype(jnp.bfloat16)
        return (slot_out, slot_in_grad, up_grad, down_grad)
    slot_out, slot_in_grad, up_grad, down_grad = lax.map(expert, (in_by_expert, cot_by_expert, up_weight, down_weight))
    out_blocks = slot_out.reshape(EXPERTS, blocks, CAP, D).transpose(1, 0, 2, 3).reshape(blocks, EXPERTS * CAP, D)
    grad_blocks = slot_in_grad.reshape(EXPERTS, blocks, CAP, D).transpose(1, 0, 2, 3).reshape(blocks, EXPERTS * CAP, D)

    def combine_block(inputs):
        hidden_rows, cot_rows, picker, weigher, out_rows, grad_rows = inputs
        gathered_out = jnp.dot(weigher.T, out_rows.astype(jnp.float32), precision=lax.Precision.HIGHEST)
        gathered_grad = jnp.dot(picker.T, grad_rows.astype(jnp.float32), precision=lax.Precision.HIGHEST)
        layer_rows = (hidden_rows.astype(jnp.float32) + gathered_out).astype(jnp.bfloat16)
        grad_back = (cot_rows.astype(jnp.float32) + gathered_grad).astype(jnp.bfloat16)
        return (layer_rows, grad_back)
    layer_out, input_grad = lax.map(combine_block, (hidden_blocks, cot_blocks, pickers, weighers, out_blocks, grad_blocks))
    return (layer_out.reshape(SEQS, LEN, D), input_grad.reshape(SEQS, LEN, D), up_grad, down_grad)
```

```python
import functools
import math

import jax
import jax.numpy as jnp
from jax import lax
from jax.experimental import pallas as pl
from jax.experimental.pallas import tpu as pltpu
from jax.sharding import PartitionSpec as P

LAT = 512
HEADS = 2
CAP = 4
BLOCK = 128
MSG = 16
MESH = pl.DeviceIdType.MESH


def group_of(kind):
    ctx_count = lax.axis_size("ctx")
    exp_count = lax.axis_size("exp")
    c = lax.axis_index("ctx")
    e = lax.axis_index("exp")
    if kind == "all":
        return (
            ctx_count * exp_count,
            c * exp_count + e,
            lambda j: (j // exp_count, j % exp_count),
        )
    if kind == "ctx":
        return ctx_count, c, lambda j: (j, e)
    if kind == "core":
        return 2, c % 2, lambda j: ((c // 2) * 2 + j, e)
    return ctx_count // 2, c // 2, lambda j: (j * 2 + c % 2, e)


def exchange_kernel(kind, same, send_ref, out_ref, send_sem, recv_sem, own_sem):
    n, me, place = group_of(kind)
    barrier = pltpu.get_barrier_semaphore()

    def greet(k, carry):
        pl.semaphore_signal(
            barrier, inc=1, device_id=place((me + k) % n), device_id_type=MESH
        )
        return carry

    lax.fori_loop(1, n, greet, 0)
    pl.semaphore_wait(barrier, n - 1)

    def copy_to(k):
        peer = (me + k) % n
        return pltpu.make_async_remote_copy(
            src_ref=send_ref if same else send_ref.at[peer],
            dst_ref=out_ref.at[me],
            send_sem=send_sem.at[k],
            recv_sem=recv_sem.at[k],
            device_id=place(peer),
            device_id_type=MESH,
        )

    def start(k, carry):
        copy_to(k).start()
        return carry

    def finish(k, carry):
        copy_to(k).wait()
        return carry

    lax.fori_loop(1, n, start, 0)
    own = pltpu.make_async_copy(
        send_ref if same else send_ref.at[me], out_ref.at[me], own_sem
    )
    own.start()
    own.wait()
    lax.fori_loop(1, n, finish, 0)


def exchange(kind, send, same, collective_id):
    n = group_of(kind)[0]
    block = send.shape if same else send.shape[1:]
    return pl.pallas_call(
        functools.partial(exchange_kernel, kind, same),
        out_shape=jax.ShapeDtypeStruct((n,) + tuple(block), send.dtype),
        in_specs=[pl.BlockSpec(memory_space=pl.ANY)],
        out_specs=pl.BlockSpec(memory_space=pl.ANY),
        scratch_shapes=[
            pltpu.SemaphoreType.DMA((n,)),
            pltpu.SemaphoreType.DMA((n,)),
            pltpu.SemaphoreType.DMA,
        ],
        compiler_params=pltpu.CompilerParams(
            collective_id=collective_id, has_side_effects=True
        ),
    )(send)


def dot32(a, b):
    return jnp.dot(a, b, preferred_element_type=jnp.float32)


def dims(a, b, contract):
    return lax.dot_general(a, b, (contract, ((), ())), preferred_element_type=jnp.float32)


def head_slice(queries, latent, doc_row, width):
    ctx_count = lax.axis_size("ctx")
    tokens = latent.shape[0]
    length = ctx_count * tokens
    send = jnp.stack(
        [
            jnp.concatenate(
                [latent, queries[:, (j * width // LAT) * LAT : (j * width // LAT + 1) * LAT]]
            )
            for j in range(ctx_count)
        ]
    )
    got = exchange("ctx", send, False, 1)
    keys = got[:, :tokens].reshape(length, LAT)
    asks = got[:, tokens:].reshape(length, LAT)
    positions = jnp.arange(length, dtype=jnp.int32)
    owner = jnp.repeat(doc_row, BLOCK, total_repeat_length=length)
    allowed = (owner[:, None] == owner[None, :]) & (positions[None, :] <= positions[:, None])
    scores = dims(asks, keys, ((1,), (1,))) * (1.0 / math.sqrt(LAT))
    scores = jnp.where(allowed, scores, -1e30)
    largest = jnp.max(scores, axis=1, keepdims=True)
    expo = jnp.where(allowed, jnp.exp(scores - largest), 0.0)
    total = jnp.sum(expo, axis=1, keepdims=True)
    first = (lax.axis_index("ctx") * width) % LAT
    values = lax.dynamic_slice(keys, (0, first), (length, width))
    return (dot32(expo.astype(jnp.bfloat16), values) / total).astype(jnp.bfloat16)


def slot_tables(route_rows, gate_rows, experts):
    tokens = route_rows.shape[0]
    named = route_rows[None, :, :] == jnp.arange(experts, dtype=jnp.int32)[:, None, None]
    hit = jnp.sum(named.astype(jnp.float32), axis=2)
    gate = jnp.sum(jnp.where(named, gate_rows[None, :, :], 0.0), axis=2)
    at = jnp.arange(tokens, dtype=jnp.int32)
    earlier = (at[:, None] < at[None, :]).astype(jnp.bfloat16)
    before = dot32(hit.astype(jnp.bfloat16), earlier)
    slots = jnp.arange(CAP, dtype=jnp.float32)
    picked = (hit[:, None, :] > 0.5) & (before[:, None, :] == slots[None, :, None])
    picker = picked.astype(jnp.float32).reshape(experts * CAP, tokens)
    weigher = jnp.where(picked, gate[:, None, :], 0.0).reshape(experts * CAP, tokens)
    return picker, weigher


def shards(
    residual,
    queries,
    latent,
    out_proj,
    up_weight,
    down_weight,
    cotangent,
    routes,
    gate_values,
    documents,
):
    ctx_count = lax.axis_size("ctx")
    experts = lax.axis_size("exp")
    tokens = residual.shape[1]
    model = residual.shape[2]
    chips = ctx_count // 2
    part = model // ctx_count
    half = part // 2
    rows = experts * CAP
    bf16 = jnp.bfloat16

    width = out_proj.shape[0]
    heads = head_slice(queries[0], latent[0], documents[0], width)
    heads = heads.reshape(chips, 2, tokens, width).swapaxes(0, 1)
    partial_sums = dot32(heads.reshape(-1, width), out_proj).astype(bf16)
    paired = exchange("core", partial_sums.reshape(2, chips * tokens, model), False, 2)
    paired = (paired[0].astype(jnp.float32) + paired[1].astype(jnp.float32)).astype(bf16)
    landed = exchange("chip", paired.reshape(chips, tokens, model), False, 3)
    projected = jnp.sum(landed.astype(jnp.float32), axis=0)
    hidden_in = (residual[0].astype(jnp.float32) + projected).astype(bf16)

    picker, weigher = slot_tables(routes[0], gate_values[0], experts)
    picker_half = picker.astype(bf16)
    slot_gate = jnp.sum(weigher, axis=1)
    slot_in = dot32(picker_half, hidden_in).astype(bf16)
    slot_cot = (dot32(picker_half, cotangent[0]) * slot_gate[:, None]).astype(bf16)

    to_row = jnp.arange(experts * MSG, dtype=jnp.int32)
    from_row = ((to_row % MSG) // CAP) * rows + (to_row // MSG) * CAP + to_row % CAP
    order = (from_row[:, None] == to_row[None, :]).astype(bf16)

    def pack(first, second):
        return jnp.einsum(
            "pq,gqw->gpw", order, jnp.concatenate([first[0], first[1], second[0], second[1]], axis=1),
            preferred_element_type=jnp.float32,
        ).astype(bf16).reshape(ctx_count * experts, MSG, half)

    def unpack(messages):
        return jnp.einsum(
            "qp,gqw->gpw", order, messages.reshape(ctx_count, experts * MSG, half),
            preferred_element_type=jnp.float32,
        ).astype(bf16)

    def by_part(values):
        return [
            jnp.stack(
                [values[:, j * part + h * half : j * part + (h + 1) * half] for j in range(ctx_count)]
            )
            for h in range(2)
        ]

    arrived = unpack(exchange("all", pack(by_part(slot_in), by_part(slot_cot)), False, 4))

    def joined(values, first):
        pieces = [
            values[:, (first + h) * rows : (first + h + 1) * rows].reshape(ctx_count * rows, half)
            for h in range(2)
        ]
        return jnp.concatenate(pieces, axis=1)

    in_rows = joined(arrived, 0)
    cot_rows = joined(arrived, 2)
    up_part = up_weight[0]
    down_part = down_weight[0]
    hidden = up_part.shape[1]

    pre_part = dot32(in_rows, up_part).astype(bf16).reshape(ctx_count, rows, hidden)
    act_part = dims(cot_rows, down_part, ((1,), (1,))).astype(bf16)
    act_part = act_part.reshape(ctx_count, rows, hidden)
    terms = exchange("ctx", jnp.concatenate([pre_part, act_part], axis=1), False, 5)
    sums = jnp.sum(terms.astype(jnp.float32), axis=0)
    pre = sums[:rows]
    act_grad = sums[rows:]
    sig = jax.nn.sigmoid(pre)
    own_act = jax.nn.silu(pre).astype(bf16)
    own_grad = (act_grad * (sig * (1.0 + pre * (1.0 - sig)))).astype(bf16)
    units = exchange("ctx", jnp.concatenate([own_act, own_grad]), True, 6)
    activated = units[:, :rows].reshape(ctx_count * rows, hidden)
    pre_grad = units[:, rows:].reshape(ctx_count * rows, hidden)

    slot_out = dot32(activated, down_part).astype(bf16)
    slot_in_grad = dims(pre_grad, up_part, ((1,), (1,))).astype(bf16)
    down_grad = dims(activated, cot_rows, ((0,), (0,))).astype(bf16)
    up_grad = dims(in_rows, pre_grad, ((0,), (0,))).astype(bf16)

    def halves(values):
        grouped = values.reshape(ctx_count, rows, part)
        return [grouped[:, :, :half], grouped[:, :, half:]]

    back = unpack(exchange("all", pack(halves(slot_out), halves(slot_in_grad)), False, 7))

    def widened(first):
        return jnp.concatenate(
            [
                back[j, (first + h) * rows : (first + h + 1) * rows]
                for j in range(ctx_count)
                for h in range(2)
            ],
            axis=1,
        )

    flat_out = widened(0)
    flat_grad = widened(2)
    high = weigher.astype(bf16)
    low = (weigher - high.astype(jnp.float32)).astype(bf16)
    gathered_out = dims(
        jnp.concatenate([high, low]), jnp.concatenate([flat_out, flat_out]), ((0,), (0,))
    )
    gathered_grad = dims(picker_half, flat_grad, ((0,), (0,)))
    layer_out = (hidden_in.astype(jnp.float32) + gathered_out).astype(bf16)
    input_grad = (cotangent[0].astype(jnp.float32) + gathered_grad).astype(bf16)
    return (layer_out[None], input_grad[None], up_grad[None], down_grad[None])


def solution(mesh):
    placed = (
        P("exp", "ctx", None),
        P("exp", "ctx", None),
        P("exp", "ctx", None),
        P("ctx", None),
        P("exp", "ctx", None),
        P("exp", None, "ctx"),
        P("exp", "ctx", None),
        P("exp", "ctx", None),
        P("exp", "ctx", None),
        P("exp", None),
    )
    return jax.shard_map(
        shards,
        mesh=mesh,
        in_specs=placed,
        out_specs=(
            P("exp", "ctx", None),
            P("exp", "ctx", None),
            P("exp", "ctx", None),
            P("exp", None, "ctx"),
        ),
        check_vma=False,
    )
```

```python
import functools
import math

import jax
import jax.numpy as jnp
from jax import lax
from jax.experimental import pallas as pl
from jax.experimental.pallas import tpu as pltpu
from jax.sharding import PartitionSpec as P

LAT = 512
HEADS = 2
CAP = 4
BLOCK = 128
MSG = 16
MESH = pl.DeviceIdType.MESH


def group_of(kind):
    ctx_count = lax.axis_size("ctx")
    exp_count = lax.axis_size("exp")
    c = lax.axis_index("ctx")
    e = lax.axis_index("exp")
    if kind == "all":
        return (
            ctx_count * exp_count,
            c * exp_count + e,
            lambda j: (j // exp_count, j % exp_count),
        )
    if kind == "ctx":
        return ctx_count, c, lambda j: (j, e)
    if kind == "core":
        return 2, c % 2, lambda j: ((c // 2) * 2 + j, e)
    return ctx_count // 2, c // 2, lambda j: (j * 2 + c % 2, e)


def exchange_kernel(jobs, *refs):
    count = len(jobs)
    sends, outs = refs[:count], refs[count : 2 * count]
    send_sems, recv_sems = refs[2 * count : 3 * count], refs[3 * count :]
    widest = "all" if any(kind == "all" for kind, _ in jobs) else jobs[0][0]
    n, me, place = group_of(widest)
    barrier = pltpu.get_barrier_semaphore()

    def greet(k, carry):
        pl.semaphore_signal(
            barrier, inc=1, device_id=place((me + k) % n), device_id_type=MESH
        )
        return carry

    lax.fori_loop(1, n, greet, 0)
    pl.semaphore_wait(barrier, n - 1)

    def copier(job):
        kind, same = jobs[job]
        n, me, place = group_of(kind)

        def copy_to(k):
            peer = (me + k) % n
            return pltpu.make_async_remote_copy(
                src_ref=sends[job] if same else sends[job].at[peer],
                dst_ref=outs[job].at[me],
                send_sem=send_sems[job].at[k],
                recv_sem=recv_sems[job].at[k],
                device_id=place(peer),
                device_id_type=MESH,
            )

        def start(k, carry):
            copy_to(k).start()
            return carry

        def finish(k, carry):
            copy_to(k).wait()
            return carry

        return n, start, finish

    for job in range(count):
        n, start, _ = copier(job)
        lax.fori_loop(1, n, start, 0)
    for job in range(count):
        n, _, finish = copier(job)
        lax.fori_loop(1, n, finish, 0)


def exchange_raw(jobs, sends, collective_id):
    sizes = [group_of(kind)[0] for kind, _ in jobs]
    blocks = [send.shape if same else send.shape[1:] for (_, same), send in zip(jobs, sends)]
    return pl.pallas_call(
        functools.partial(exchange_kernel, tuple(jobs)),
        out_shape=[
            jax.ShapeDtypeStruct((n,) + tuple(block), send.dtype)
            for n, block, send in zip(sizes, blocks, sends)
        ],
        in_specs=[pl.BlockSpec(memory_space=pl.ANY)] * len(jobs),
        out_specs=[pl.BlockSpec(memory_space=pl.ANY)] * len(jobs),
        scratch_shapes=[pltpu.SemaphoreType.DMA((n,)) for n in sizes] * 2,
        compiler_params=pltpu.CompilerParams(
            collective_id=collective_id, has_side_effects=True
        ),
    )(*sends)


def with_own(kind, same, send, got):
    n, me, _ = group_of(kind)
    mine = jnp.arange(n).reshape((n,) + (1,) * (got.ndim - 1)) == me
    return jnp.where(mine, send[None] if same else send, got)


def exchange(kind, send, same, collective_id):
    (got,) = exchange_raw([(kind, same)], [send], collective_id)
    return with_own(kind, same, send, got)


def dot32(a, b):
    return jnp.dot(a, b, preferred_element_type=jnp.float32)


def dims(a, b, contract):
    return lax.dot_general(a, b, (contract, ((), ())), preferred_element_type=jnp.float32)


def head_inputs(queries, latent, width):
    ctx_count = lax.axis_size("ctx")
    return jnp.stack(
        [
            jnp.concatenate(
                [latent, queries[:, (j * width // LAT) * LAT : (j * width // LAT + 1) * LAT]]
            )
            for j in range(ctx_count)
        ]
    )


def head_slice(got, doc_row, width):
    tokens = got.shape[1] // 2
    length = got.shape[0] * tokens
    keys = got[:, :tokens].reshape(length, LAT)
    asks = got[:, tokens:].reshape(length, LAT)
    positions = jnp.arange(length, dtype=jnp.int32)
    owner = jnp.repeat(doc_row, BLOCK, total_repeat_length=length)
    allowed = (owner[:, None] == owner[None, :]) & (positions[None, :] <= positions[:, None])
    scores = dims(asks, keys, ((1,), (1,))) * (1.0 / math.sqrt(LAT))
    scores = jnp.where(allowed, scores, -1e30)
    largest = jnp.max(scores, axis=1, keepdims=True)
    expo = jnp.where(allowed, jnp.exp(scores - largest), 0.0)
    total = jnp.sum(expo, axis=1, keepdims=True)
    first = (lax.axis_index("ctx") * width) % LAT
    values = lax.dynamic_slice(keys, (0, first), (length, width))
    return (dot32(expo.astype(jnp.bfloat16), values) / total).astype(jnp.bfloat16)


def slot_tables(route_rows, gate_rows, experts):
    tokens = route_rows.shape[0]
    named = route_rows[None, :, :] == jnp.arange(experts, dtype=jnp.int32)[:, None, None]
    hit = jnp.sum(named.astype(jnp.float32), axis=2)
    gate = jnp.sum(jnp.where(named, gate_rows[None, :, :], 0.0), axis=2)
    at = jnp.arange(tokens, dtype=jnp.int32)
    earlier = (at[:, None] < at[None, :]).astype(jnp.bfloat16)
    before = dot32(hit.astype(jnp.bfloat16), earlier)
    slots = jnp.arange(CAP, dtype=jnp.float32)
    picked = (hit[:, None, :] > 0.5) & (before[:, None, :] == slots[None, :, None])
    picker = picked.astype(jnp.float32).reshape(experts * CAP, tokens)
    weigher = jnp.where(picked, gate[:, None, :], 0.0).reshape(experts * CAP, tokens)
    return picker, weigher


def shards(
    residual,
    queries,
    latent,
    out_proj,
    up_weight,
    down_weight,
    cotangent,
    routes,
    gate_values,
    documents,
):
    ctx_count = lax.axis_size("ctx")
    experts = lax.axis_size("exp")
    tokens = residual.shape[1]
    model = residual.shape[2]
    chips = ctx_count // 2
    part = model // ctx_count
    half = part // 2
    rows = experts * CAP
    bf16 = jnp.bfloat16

    picker, weigher = slot_tables(routes[0], gate_values[0], experts)
    picker_half = picker.astype(bf16)
    slot_gate = jnp.sum(weigher, axis=1)
    slot_cot = (dot32(picker_half, cotangent[0]) * slot_gate[:, None]).astype(bf16)

    to_row = jnp.arange(experts * MSG, dtype=jnp.int32)
    from_row = ((to_row % MSG) // CAP) * rows + (to_row // MSG) * CAP + to_row % CAP
    order = (from_row[:, None] == to_row[None, :]).astype(bf16)

    def pack(pieces):
        packed = jnp.einsum(
            "pq,gqw->gpw", order, jnp.concatenate(pieces, axis=1),
            preferred_element_type=jnp.float32,
        )
        return packed.astype(bf16).reshape(ctx_count * experts, MSG, -1)

    def unpack(messages):
        return jnp.einsum(
            "qp,gqw->gpw", order, messages.reshape(ctx_count, experts * MSG, -1),
            preferred_element_type=jnp.float32,
        ).astype(bf16)

    quarter = part // 4

    def by_part(values):
        return [
            jnp.stack(
                [
                    values[:, j * part + q * quarter : j * part + (q + 1) * quarter]
                    for j in range(ctx_count)
                ]
            )
            for q in range(4)
        ]

    def joined(values):
        pieces = [
            values[:, q * rows : (q + 1) * rows].reshape(ctx_count * rows, quarter)
            for q in range(4)
        ]
        return jnp.concatenate(pieces, axis=1)

    width = out_proj.shape[0]
    head_send = head_inputs(queries[0], latent[0], width)
    cot_send = pack(by_part(slot_cot))
    head_got, cot_got = exchange_raw(
        [("ctx", False), ("all", False)], [head_send, cot_send], 1
    )
    cot_rows = joined(unpack(with_own("all", False, cot_send, cot_got)))

    heads = head_slice(with_own("ctx", False, head_send, head_got), documents[0], width)
    heads = heads.reshape(chips, 2, tokens, width).swapaxes(0, 1)
    partial_sums = dot32(heads.reshape(-1, width), out_proj).astype(bf16)
    partial_sums = partial_sums.reshape(2, chips * tokens, model)
    (paired,) = exchange_raw([("core", False)], [partial_sums], 2)
    core = lax.axis_index("ctx") % 2
    paired = (
        lax.dynamic_index_in_dim(partial_sums, core, 0, False).astype(jnp.float32)
        + lax.dynamic_index_in_dim(paired, 1 - core, 0, False).astype(jnp.float32)
    ).astype(bf16)
    landed = exchange("chip", paired.reshape(chips, tokens, model), False, 3)
    projected = jnp.sum(landed.astype(jnp.float32), axis=0)
    hidden_in = (residual[0].astype(jnp.float32) + projected).astype(bf16)
    slot_in = dot32(picker_half, hidden_in).astype(bf16)
    in_rows = joined(unpack(exchange("all", pack(by_part(slot_in)), False, 4)))
    up_part = up_weight[0]
    down_part = down_weight[0]
    hidden = up_part.shape[1]

    pre_part = dot32(in_rows, up_part).astype(bf16).reshape(ctx_count, rows, hidden)
    act_part = dims(cot_rows, down_part, ((1,), (1,))).astype(bf16)
    act_part = act_part.reshape(ctx_count, rows, hidden)
    terms = exchange("ctx", jnp.concatenate([pre_part, act_part], axis=1), False, 5)
    sums = jnp.sum(terms.astype(jnp.float32), axis=0)
    pre = sums[:rows]
    act_grad = sums[rows:]
    sig = jax.nn.sigmoid(pre)
    own_act = jax.nn.silu(pre).astype(bf16)
    own_grad = (act_grad * (sig * (1.0 + pre * (1.0 - sig)))).astype(bf16)
    units = exchange("ctx", jnp.concatenate([own_act, own_grad]), True, 6)
    activated = units[:, :rows].reshape(ctx_count * rows, hidden)
    pre_grad = units[:, rows:].reshape(ctx_count * rows, hidden)

    slot_out = dot32(activated, down_part).astype(bf16)
    slot_in_grad = dims(pre_grad, up_part, ((1,), (1,))).astype(bf16)
    down_grad = dims(activated, cot_rows, ((0,), (0,))).astype(bf16)
    up_grad = dims(in_rows, pre_grad, ((0,), (0,))).astype(bf16)

    def halves(values):
        grouped = values.reshape(ctx_count, rows, part)
        return [grouped[:, :, :half], grouped[:, :, half:]]

    back = unpack(exchange("all", pack(halves(slot_out) + halves(slot_in_grad)), False, 7))

    def widened(first):
        return jnp.concatenate(
            [
                back[j, (first + h) * rows : (first + h + 1) * rows]
                for j in range(ctx_count)
                for h in range(2)
            ],
            axis=1,
        )

    flat_out = widened(0)
    flat_grad = widened(2)
    high = weigher.astype(bf16)
    low = (weigher - high.astype(jnp.float32)).astype(bf16)
    gathered_out = dims(
        jnp.concatenate([high, low]), jnp.concatenate([flat_out, flat_out]), ((0,), (0,))
    )
    gathered_grad = dims(picker_half, flat_grad, ((0,), (0,)))
    layer_out = (hidden_in.astype(jnp.float32) + gathered_out).astype(bf16)
    input_grad = (cotangent[0].astype(jnp.float32) + gathered_grad).astype(bf16)
    return (layer_out[None], input_grad[None], up_grad[None], down_grad[None])


def solution(mesh):
    placed = (
        P("exp", "ctx", None),
        P("exp", "ctx", None),
        P("exp", "ctx", None),
        P("ctx", None),
        P("exp", "ctx", None),
        P("exp", None, "ctx"),
        P("exp", "ctx", None),
        P("exp", "ctx", None),
        P("exp", "ctx", None),
        P("exp", None),
    )
    return jax.shard_map(
        shards,
        mesh=mesh,
        in_specs=placed,
        out_specs=(
            P("exp", "ctx", None),
            P("exp", "ctx", None),
            P("exp", "ctx", None),
            P("exp", None, "ctx"),
        ),
        check_vma=False,
    )
```

```python
import functools
import math

import jax
import jax.numpy as jnp
from jax import lax
from jax.experimental import pallas as pl
from jax.experimental.pallas import tpu as pltpu
from jax.sharding import PartitionSpec as P

LAT = 512
HEADS = 2
CAP = 4
BLOCK = 128
MSG = 16
MESH = pl.DeviceIdType.MESH


def group_of(kind):
    ctx_count = lax.axis_size("ctx")
    exp_count = lax.axis_size("exp")
    c = lax.axis_index("ctx")
    e = lax.axis_index("exp")
    if kind == "all":
        return (
            ctx_count * exp_count,
            c * exp_count + e,
            lambda j: (j // exp_count, j % exp_count),
        )
    if kind == "ctx":
        return ctx_count, c, lambda j: (j, e)
    if kind == "core":
        return 2, c % 2, lambda j: ((c // 2) * 2 + j, e)
    return ctx_count // 2, c // 2, lambda j: (j * 2 + c % 2, e)


def exchange_kernel(jobs, *refs):
    count = len(jobs)
    sends, outs = refs[:count], refs[count : 2 * count]
    send_sems, recv_sems = refs[2 * count : 3 * count], refs[3 * count :]
    widest = "all" if any(kind == "all" for kind, _ in jobs) else jobs[0][0]
    n, me, place = group_of(widest)
    barrier = pltpu.get_barrier_semaphore()

    def greet(k, carry):
        pl.semaphore_signal(
            barrier, inc=1, device_id=place((me + k) % n), device_id_type=MESH
        )
        return carry

    lax.fori_loop(1, n, greet, 0)
    pl.semaphore_wait(barrier, n - 1)

    def copier(job):
        kind, same = jobs[job]
        n, me, place = group_of(kind)

        def copy_to(k):
            peer = (me + k) % n
            return pltpu.make_async_remote_copy(
                src_ref=sends[job] if same else sends[job].at[peer],
                dst_ref=outs[job].at[me],
                send_sem=send_sems[job].at[k],
                recv_sem=recv_sems[job].at[k],
                device_id=place(peer),
                device_id_type=MESH,
            )

        def start(k, carry):
            copy_to(k).start()
            return carry

        def finish(k, carry):
            copy_to(k).wait()
            return carry

        return n, start, finish

    for job in range(count):
        n, start, _ = copier(job)
        lax.fori_loop(1, n, start, 0)
    for job in range(count):
        n, _, finish = copier(job)
        lax.fori_loop(1, n, finish, 0)


def exchange_raw(jobs, sends, collective_id):
    sizes = [group_of(kind)[0] for kind, _ in jobs]
    blocks = [send.shape if same else send.shape[1:] for (_, same), send in zip(jobs, sends)]
    return pl.pallas_call(
        functools.partial(exchange_kernel, tuple(jobs)),
        out_shape=[
            jax.ShapeDtypeStruct((n,) + tuple(block), send.dtype)
            for n, block, send in zip(sizes, blocks, sends)
        ],
        in_specs=[pl.BlockSpec(memory_space=pl.ANY)] * len(jobs),
        out_specs=[pl.BlockSpec(memory_space=pl.ANY)] * len(jobs),
        scratch_shapes=[pltpu.SemaphoreType.DMA((n,)) for n in sizes] * 2,
        compiler_params=pltpu.CompilerParams(
            collective_id=collective_id, has_side_effects=True
        ),
    )(*sends)


def with_own(kind, same, send, got):
    n, me, _ = group_of(kind)
    mine = jnp.arange(n).reshape((n,) + (1,) * (got.ndim - 1)) == me
    return jnp.where(mine, send[None] if same else send, got)


def exchange(kind, send, same, collective_id):
    (got,) = exchange_raw([(kind, same)], [send], collective_id)
    return with_own(kind, same, send, got)


def dot32(a, b):
    return jnp.dot(a, b, preferred_element_type=jnp.float32)


def dims(a, b, contract):
    return lax.dot_general(a, b, (contract, ((), ())), preferred_element_type=jnp.float32)


def head_inputs(queries, latent, width):
    ctx_count = lax.axis_size("ctx")
    return jnp.stack(
        [
            jnp.concatenate(
                [latent, queries[:, (j * width // LAT) * LAT : (j * width // LAT + 1) * LAT]]
            )
            for j in range(ctx_count)
        ]
    )


def head_slice(got, doc_row, width):
    tokens = got.shape[1] // 2
    length = got.shape[0] * tokens
    keys = got[:, :tokens].reshape(length, LAT)
    asks = got[:, tokens:].reshape(length, LAT)
    positions = jnp.arange(length, dtype=jnp.int32)
    owner = jnp.repeat(doc_row, BLOCK, total_repeat_length=length)
    allowed = (owner[:, None] == owner[None, :]) & (positions[None, :] <= positions[:, None])
    scores = dims(asks, keys, ((1,), (1,))) * (1.0 / math.sqrt(LAT))
    scores = jnp.where(allowed, scores, -1e30)
    largest = jnp.max(scores, axis=1, keepdims=True)
    expo = jnp.where(allowed, jnp.exp(scores - largest), 0.0)
    total = jnp.sum(expo, axis=1, keepdims=True)
    first = (lax.axis_index("ctx") * width) % LAT
    values = lax.dynamic_slice(keys, (0, first), (length, width))
    return (dot32(expo.astype(jnp.bfloat16), values) / total).astype(jnp.bfloat16)


def slot_tables(route_rows, gate_rows, experts):
    tokens = route_rows.shape[0]
    named = route_rows[None, :, :] == jnp.arange(experts, dtype=jnp.int32)[:, None, None]
    hit = jnp.sum(named.astype(jnp.float32), axis=2)
    gate = jnp.sum(jnp.where(named, gate_rows[None, :, :], 0.0), axis=2)
    at = jnp.arange(tokens, dtype=jnp.int32)
    earlier = (at[:, None] < at[None, :]).astype(jnp.bfloat16)
    before = dot32(hit.astype(jnp.bfloat16), earlier)
    slots = jnp.arange(CAP, dtype=jnp.float32)
    picked = (hit[:, None, :] > 0.5) & (before[:, None, :] == slots[None, :, None])
    picker = picked.astype(jnp.float32).reshape(experts * CAP, tokens)
    weigher = jnp.where(picked, gate[:, None, :], 0.0).reshape(experts * CAP, tokens)
    return picker, weigher


def shards(
    residual,
    queries,
    latent,
    out_proj,
    up_weight,
    down_weight,
    cotangent,
    routes,
    gate_values,
    documents,
):
    ctx_count = lax.axis_size("ctx")
    experts = lax.axis_size("exp")
    tokens = residual.shape[1]
    model = residual.shape[2]
    chips = ctx_count // 2
    part = model // ctx_count
    half = part // 2
    rows = experts * CAP
    bf16 = jnp.bfloat16

    picker, weigher = slot_tables(routes[0], gate_values[0], experts)
    picker_half = picker.astype(bf16)
    slot_gate = jnp.sum(weigher, axis=1)
    slot_cot = (dot32(picker_half, cotangent[0]) * slot_gate[:, None]).astype(bf16)

    to_row = jnp.arange(experts * MSG, dtype=jnp.int32)
    from_row = ((to_row % MSG) // CAP) * rows + (to_row // MSG) * CAP + to_row % CAP
    order = (from_row[:, None] == to_row[None, :]).astype(bf16)

    def pack(pieces):
        packed = jnp.einsum(
            "pq,gqw->gpw", order, jnp.concatenate(pieces, axis=1),
            preferred_element_type=jnp.float32,
        )
        return packed.astype(bf16).reshape(ctx_count * experts, MSG, -1)

    def unpack(messages):
        return jnp.einsum(
            "qp,gqw->gpw", order, messages.reshape(ctx_count, experts * MSG, -1),
            preferred_element_type=jnp.float32,
        ).astype(bf16)

    quarter = part // 4

    def by_part(values):
        return [
            jnp.stack(
                [
                    values[:, j * part + q * quarter : j * part + (q + 1) * quarter]
                    for j in range(ctx_count)
                ]
            )
            for q in range(4)
        ]

    def joined(values):
        pieces = [
            values[:, q * rows : (q + 1) * rows].reshape(ctx_count * rows, quarter)
            for q in range(4)
        ]
        return jnp.concatenate(pieces, axis=1)

    width = out_proj.shape[0]
    head_send = head_inputs(queries[0], latent[0], width)
    cot_send = pack(by_part(slot_cot))
    heads = head_slice(exchange("ctx", head_send, False, 1), documents[0], width)
    heads = heads.reshape(chips, 2, tokens, width).swapaxes(0, 1)
    partial_sums = dot32(heads.reshape(-1, width), out_proj).astype(bf16)
    partial_sums = partial_sums.reshape(2, chips * tokens, model)
    (paired,) = exchange_raw([("core", False)], [partial_sums], 2)
    core = lax.axis_index("ctx") % 2
    paired = (
        lax.dynamic_index_in_dim(partial_sums, core, 0, False).astype(jnp.float32)
        + lax.dynamic_index_in_dim(paired, 1 - core, 0, False).astype(jnp.float32)
    ).astype(bf16)
    paired = paired.reshape(chips, tokens, model)
    landed, cot_got = exchange_raw(
        [("chip", False), ("all", False)], [paired, cot_send], 3
    )
    landed = with_own("chip", False, paired, landed)
    cot_rows = joined(unpack(with_own("all", False, cot_send, cot_got)))
    projected = jnp.sum(landed.astype(jnp.float32), axis=0)
    hidden_in = (residual[0].astype(jnp.float32) + projected).astype(bf16)
    slot_in = dot32(picker_half, hidden_in).astype(bf16)
    in_rows = joined(unpack(exchange("all", pack(by_part(slot_in)), False, 4)))
    up_part = up_weight[0]
    down_part = down_weight[0]
    hidden = up_part.shape[1]

    pre_part = dot32(in_rows, up_part).astype(bf16).reshape(ctx_count, rows, hidden)
    act_part = dims(cot_rows, down_part, ((1,), (1,))).astype(bf16)
    act_part = act_part.reshape(ctx_count, rows, hidden)
    terms = exchange("ctx", jnp.concatenate([pre_part, act_part], axis=1), False, 5)
    sums = jnp.sum(terms.astype(jnp.float32), axis=0)
    pre = sums[:rows]
    act_grad = sums[rows:]
    sig = jax.nn.sigmoid(pre)
    own_act = jax.nn.silu(pre).astype(bf16)
    own_grad = (act_grad * (sig * (1.0 + pre * (1.0 - sig)))).astype(bf16)
    units = exchange("ctx", jnp.concatenate([own_act, own_grad]), True, 6)
    activated = units[:, :rows].reshape(ctx_count * rows, hidden)
    pre_grad = units[:, rows:].reshape(ctx_count * rows, hidden)

    slot_out = dot32(activated, down_part).astype(bf16)
    slot_in_grad = dims(pre_grad, up_part, ((1,), (1,))).astype(bf16)
    down_grad = dims(activated, cot_rows, ((0,), (0,))).astype(bf16)
    up_grad = dims(in_rows, pre_grad, ((0,), (0,))).astype(bf16)

    def halves(values):
        grouped = values.reshape(ctx_count, rows, part)
        return [grouped[:, :, :half], grouped[:, :, half:]]

    back = unpack(exchange("all", pack(halves(slot_out) + halves(slot_in_grad)), False, 7))

    def widened(first):
        return jnp.concatenate(
            [
                back[j, (first + h) * rows : (first + h + 1) * rows]
                for j in range(ctx_count)
                for h in range(2)
            ],
            axis=1,
        )

    flat_out = widened(0)
    flat_grad = widened(2)
    high = weigher.astype(bf16)
    low = (weigher - high.astype(jnp.float32)).astype(bf16)
    gathered_out = dims(
        jnp.concatenate([high, low]), jnp.concatenate([flat_out, flat_out]), ((0,), (0,))
    )
    gathered_grad = dims(picker_half, flat_grad, ((0,), (0,)))
    layer_out = (hidden_in.astype(jnp.float32) + gathered_out).astype(bf16)
    input_grad = (cotangent[0].astype(jnp.float32) + gathered_grad).astype(bf16)
    return (layer_out[None], input_grad[None], up_grad[None], down_grad[None])


def solution(mesh):
    placed = (
        P("exp", "ctx", None),
        P("exp", "ctx", None),
        P("exp", "ctx", None),
        P("ctx", None),
        P("exp", "ctx", None),
        P("exp", None, "ctx"),
        P("exp", "ctx", None),
        P("exp", "ctx", None),
        P("exp", "ctx", None),
        P("exp", None),
    )
    return jax.shard_map(
        shards,
        mesh=mesh,
        in_specs=placed,
        out_specs=(
            P("exp", "ctx", None),
            P("exp", "ctx", None),
            P("exp", "ctx", None),
            P("exp", None, "ctx"),
        ),
        check_vma=False,
    )
```

```python
import functools
import math

import jax
import jax.numpy as jnp
from jax import lax
from jax.experimental import pallas as pl
from jax.experimental.pallas import tpu as pltpu
from jax.sharding import PartitionSpec as P

LAT = 512
HEADS = 2
CAP = 4
BLOCK = 128
MSG = 16
MESH = pl.DeviceIdType.MESH


def group_of(kind):
    ctx_count = lax.axis_size("ctx")
    exp_count = lax.axis_size("exp")
    c = lax.axis_index("ctx")
    e = lax.axis_index("exp")
    if kind == "all":
        return (
            ctx_count * exp_count,
            c * exp_count + e,
            lambda j: (j // exp_count, j % exp_count),
        )
    if kind == "ctx":
        return ctx_count, c, lambda j: (j, e)
    if kind == "core":
        return 2, c % 2, lambda j: ((c // 2) * 2 + j, e)
    return ctx_count // 2, c // 2, lambda j: (j * 2 + c % 2, e)


def exchange_kernel(jobs, *refs):
    count = len(jobs)
    sends, outs = refs[:count], refs[count : 2 * count]
    send_sems, recv_sems = refs[2 * count : 3 * count], refs[3 * count :]
    widest = "all" if any(kind == "all" for kind, _ in jobs) else jobs[0][0]
    n, me, place = group_of(widest)
    barrier = pltpu.get_barrier_semaphore()

    def greet(k, carry):
        pl.semaphore_signal(
            barrier, inc=1, device_id=place((me + k) % n), device_id_type=MESH
        )
        return carry

    lax.fori_loop(1, n, greet, 0)
    pl.semaphore_wait(barrier, n - 1)

    def copier(job):
        kind, same = jobs[job]
        n, me, place = group_of(kind)

        def copy_to(k):
            peer = (me + k) % n
            return pltpu.make_async_remote_copy(
                src_ref=sends[job] if same else sends[job].at[peer],
                dst_ref=outs[job].at[me],
                send_sem=send_sems[job].at[k],
                recv_sem=recv_sems[job].at[k],
                device_id=place(peer),
                device_id_type=MESH,
            )

        def start(k, carry):
            copy_to(k).start()
            return carry

        def finish(k, carry):
            copy_to(k).wait()
            return carry

        return n, start, finish

    for job in range(count):
        n, start, _ = copier(job)
        lax.fori_loop(1, n, start, 0)
    for job in range(count):
        n, _, finish = copier(job)
        lax.fori_loop(1, n, finish, 0)


def exchange_raw(jobs, sends, collective_id):
    sizes = [group_of(kind)[0] for kind, _ in jobs]
    blocks = [send.shape if same else send.shape[1:] for (_, same), send in zip(jobs, sends)]
    return pl.pallas_call(
        functools.partial(exchange_kernel, tuple(jobs)),
        out_shape=[
            jax.ShapeDtypeStruct((n,) + tuple(block), send.dtype)
            for n, block, send in zip(sizes, blocks, sends)
        ],
        in_specs=[pl.BlockSpec(memory_space=pl.ANY)] * len(jobs),
        out_specs=[pl.BlockSpec(memory_space=pl.ANY)] * len(jobs),
        scratch_shapes=[pltpu.SemaphoreType.DMA((n,)) for n in sizes] * 2,
        compiler_params=pltpu.CompilerParams(
            collective_id=collective_id, has_side_effects=True
        ),
    )(*sends)


def with_own(kind, same, send, got):
    n, me, _ = group_of(kind)
    mine = jnp.arange(n).reshape((n,) + (1,) * (got.ndim - 1)) == me
    return jnp.where(mine, send[None] if same else send, got)


def exchange(kind, send, same, collective_id):
    (got,) = exchange_raw([(kind, same)], [send], collective_id)
    return with_own(kind, same, send, got)


def dot32(a, b):
    return jnp.dot(a, b, preferred_element_type=jnp.float32)


def dims(a, b, contract):
    return lax.dot_general(a, b, (contract, ((), ())), preferred_element_type=jnp.float32)


def head_inputs(queries, latent, width):
    ctx_count = lax.axis_size("ctx")
    return jnp.stack(
        [
            jnp.concatenate(
                [latent, queries[:, (j * width // LAT) * LAT : (j * width // LAT + 1) * LAT]]
            )
            for j in range(ctx_count)
        ]
    )


def head_slice(got, doc_row, width):
    tokens = got.shape[1] // 2
    length = got.shape[0] * tokens
    keys = got[:, :tokens].reshape(length, LAT)
    asks = got[:, tokens:].reshape(length, LAT)
    positions = jnp.arange(length, dtype=jnp.int32)
    owner = jnp.repeat(doc_row, BLOCK, total_repeat_length=length)
    allowed = (owner[:, None] == owner[None, :]) & (positions[None, :] <= positions[:, None])
    scores = dims(asks, keys, ((1,), (1,))) * (1.0 / math.sqrt(LAT))
    scores = jnp.where(allowed, scores, -1e30)
    largest = jnp.max(scores, axis=1, keepdims=True)
    expo = jnp.where(allowed, jnp.exp(scores - largest), 0.0)
    total = jnp.sum(expo, axis=1, keepdims=True)
    first = (lax.axis_index("ctx") * width) % LAT
    values = lax.dynamic_slice(keys, (0, first), (length, width))
    return (dot32(expo.astype(jnp.bfloat16), values) / total).astype(jnp.bfloat16)


def slot_tables(route_rows, gate_rows, experts):
    tokens = route_rows.shape[0]
    named = route_rows[None, :, :] == jnp.arange(experts, dtype=jnp.int32)[:, None, None]
    hit = jnp.sum(named.astype(jnp.float32), axis=2)
    gate = jnp.sum(jnp.where(named, gate_rows[None, :, :], 0.0), axis=2)
    at = jnp.arange(tokens, dtype=jnp.int32)
    earlier = (at[:, None] < at[None, :]).astype(jnp.bfloat16)
    before = dot32(hit.astype(jnp.bfloat16), earlier)
    slots = jnp.arange(CAP, dtype=jnp.float32)
    picked = (hit[:, None, :] > 0.5) & (before[:, None, :] == slots[None, :, None])
    picker = picked.astype(jnp.float32).reshape(experts * CAP, tokens)
    weigher = jnp.where(picked, gate[:, None, :], 0.0).reshape(experts * CAP, tokens)
    return picker, weigher


def shards(
    residual,
    queries,
    latent,
    out_proj,
    up_weight,
    down_weight,
    cotangent,
    routes,
    gate_values,
    documents,
):
    ctx_count = lax.axis_size("ctx")
    experts = lax.axis_size("exp")
    tokens = residual.shape[1]
    model = residual.shape[2]
    chips = ctx_count // 2
    part = model // ctx_count
    half = part // 2
    rows = experts * CAP
    bf16 = jnp.bfloat16

    picker, weigher = slot_tables(routes[0], gate_values[0], experts)
    picker_half = picker.astype(bf16)
    slot_gate = jnp.sum(weigher, axis=1)
    slot_cot = (dot32(picker_half, cotangent[0]) * slot_gate[:, None]).astype(bf16)

    to_row = jnp.arange(experts * MSG, dtype=jnp.int32)
    from_row = ((to_row % MSG) // CAP) * rows + (to_row // MSG) * CAP + to_row % CAP
    order = (from_row[:, None] == to_row[None, :]).astype(bf16)

    def pack(pieces):
        packed = jnp.einsum(
            "pq,gqw->gpw", order, jnp.concatenate(pieces, axis=1),
            preferred_element_type=jnp.float32,
        )
        return packed.astype(bf16).reshape(ctx_count * experts, MSG, -1)

    def unpack(messages):
        return jnp.einsum(
            "qp,gqw->gpw", order, messages.reshape(ctx_count, experts * MSG, -1),
            preferred_element_type=jnp.float32,
        ).astype(bf16)

    quarter = part // 4

    def by_part(values):
        return [
            jnp.stack(
                [
                    values[:, j * part + q * quarter : j * part + (q + 1) * quarter]
                    for j in range(ctx_count)
                ]
            )
            for q in range(4)
        ]

    def joined(values):
        pieces = [
            values[:, q * rows : (q + 1) * rows].reshape(ctx_count * rows, quarter)
            for q in range(4)
        ]
        return jnp.concatenate(pieces, axis=1)

    width = out_proj.shape[0]
    head_send = head_inputs(queries[0], latent[0], width)
    cot_send = pack(by_part(slot_cot))
    heads = head_slice(exchange("ctx", head_send, False, 1), documents[0], width)
    heads = heads.reshape(chips, 2, tokens, width).swapaxes(0, 1)
    partial_sums = dot32(heads.reshape(-1, width), out_proj).astype(bf16)
    partial_sums = partial_sums.reshape(2, chips * tokens, model)
    paired, cot_got = exchange_raw(
        [("core", False), ("all", False)], [partial_sums, cot_send], 2
    )
    cot_rows = joined(unpack(with_own("all", False, cot_send, cot_got)))
    core = lax.axis_index("ctx") % 2
    paired = (
        lax.dynamic_index_in_dim(partial_sums, core, 0, False).astype(jnp.float32)
        + lax.dynamic_index_in_dim(paired, 1 - core, 0, False).astype(jnp.float32)
    ).astype(bf16)
    landed = exchange("chip", paired.reshape(chips, tokens, model), False, 3)
    projected = jnp.sum(landed.astype(jnp.float32), axis=0)
    hidden_in = (residual[0].astype(jnp.float32) + projected).astype(bf16)
    slot_in = dot32(picker_half, hidden_in).astype(bf16)
    in_rows = joined(unpack(exchange("all", pack(by_part(slot_in)), False, 4)))
    up_part = up_weight[0]
    down_part = down_weight[0]
    hidden = up_part.shape[1]

    pre_part = dot32(in_rows, up_part).astype(bf16).reshape(ctx_count, rows, hidden)
    act_part = dims(cot_rows, down_part, ((1,), (1,))).astype(bf16)
    act_part = act_part.reshape(ctx_count, rows, hidden)
    terms = exchange("ctx", jnp.concatenate([pre_part, act_part], axis=1), False, 5)
    sums = jnp.sum(terms.astype(jnp.float32), axis=0)
    pre = sums[:rows]
    act_grad = sums[rows:]
    sig = jax.nn.sigmoid(pre)
    own_act = jax.nn.silu(pre).astype(bf16)
    own_grad = (act_grad * (sig * (1.0 + pre * (1.0 - sig)))).astype(bf16)
    units = exchange("ctx", jnp.concatenate([own_act, own_grad]), True, 6)
    activated = units[:, :rows].reshape(ctx_count * rows, hidden)
    pre_grad = units[:, rows:].reshape(ctx_count * rows, hidden)

    slot_out = dot32(activated, down_part).astype(bf16)
    slot_in_grad = dims(pre_grad, up_part, ((1,), (1,))).astype(bf16)
    down_grad = dims(activated, cot_rows, ((0,), (0,))).astype(bf16)
    up_grad = dims(in_rows, pre_grad, ((0,), (0,))).astype(bf16)

    def halves(values):
        grouped = values.reshape(ctx_count, rows, part)
        return [grouped[:, :, :half], grouped[:, :, half:]]

    back = unpack(exchange("all", pack(halves(slot_out) + halves(slot_in_grad)), False, 7))

    def widened(first):
        return jnp.concatenate(
            [
                back[j, (first + h) * rows : (first + h + 1) * rows]
                for j in range(ctx_count)
                for h in range(2)
            ],
            axis=1,
        )

    flat_out = widened(0)
    flat_grad = widened(2)
    high = weigher.astype(bf16)
    low = (weigher - high.astype(jnp.float32)).astype(bf16)
    gathered_out = dims(
        jnp.concatenate([high, low]), jnp.concatenate([flat_out, flat_out]), ((0,), (0,))
    )
    gathered_grad = dims(picker_half, flat_grad, ((0,), (0,)))
    layer_out = (hidden_in.astype(jnp.float32) + gathered_out).astype(bf16)
    input_grad = (cotangent[0].astype(jnp.float32) + gathered_grad).astype(bf16)
    return (layer_out[None], input_grad[None], up_grad[None], down_grad[None])


def solution(mesh):
    placed = (
        P("exp", "ctx", None),
        P("exp", "ctx", None),
        P("exp", "ctx", None),
        P("ctx", None),
        P("exp", "ctx", None),
        P("exp", None, "ctx"),
        P("exp", "ctx", None),
        P("exp", "ctx", None),
        P("exp", "ctx", None),
        P("exp", None),
    )
    return jax.shard_map(
        shards,
        mesh=mesh,
        in_specs=placed,
        out_specs=(
            P("exp", "ctx", None),
            P("exp", "ctx", None),
            P("exp", "ctx", None),
            P("exp", None, "ctx"),
        ),
        check_vma=False,
    )
```
